512 devices in a mesh: dp: 8 (over z_lo, core), gx: 4 (over x), gy: 4 (over z_hi), gz: 4 (over y).
Axes of the slice: x: 4, y: 4, z: 16 (z_hi: 4, z_lo: 4; z = z_hi * 4 + z_lo), core: 2. Of those that a mesh axis runs over, the one named last changes fastest.
Arguments:
- activations: bfloat16 [8192, 8192], P(('dp', 'gy'), 'gx'), may hold values from -0.06591797 to 0.06591797
- out_grad: bfloat16 [8192, 8192], P(('dp', 'gy'), ('gz', 'gx')), may hold values from -6 to 6
- weight: bfloat16 [8192, 8192], P(('gx', 'gy'), 'gz'), may hold values from -0.09375 to 0.09375
Outputs:
- input_grad: bfloat16 [8192, 8192], P(('dp', 'gy'), ('gx', 'gz'))
- weight_grad: float32 [8192, 8192], P(('gx', 'dp'), ('gz', 'gy'))
The draws below stay inside these ranges and needn't reach their ends.
All inputs are finite; a program needn't handle non-finite values.
Results may differ from the reference program's by a relative error of at most 0.015.
Values may be sent and summed in bfloat16 or wider, within the bound.
No kernel may reach another device: no remote copies, remote signals or barrier semaphores. Data moves between devices by JAX's collectives and lax.ppermute only.
A program may use at most 64 MiB of HBM per device.

```python
import jax
import jax.numpy as jnp
from jax import lax

D = 8192
TOKENS = 8192
N_DP = 8
N_GZ = 4


def strengthened(entries, key, source, target, shards_of, factor):
    def block_of(position):
        return (jnp.arange(entries.shape[position]) // (entries.shape[position] // shards_of)).reshape((-1,) + (1,) * (entries.ndim - 1 - position))

    first = jax.random.permutation(key, shards_of)[block_of(target)]
    other_side = (block_of(target) + shards_of // 2) % shards_of
    return jnp.where((block_of(source) == first) | (block_of(source) == other_side), factor * entries, entries)


def shard_levels(stream_key, extent, shards, least, largest):
    loudness = 1.0
    for position, blocks in shards:
        heights = jax.random.uniform(jax.random.fold_in(jax.random.fold_in(stream_key, 6), position), (blocks,), jnp.float32, least / len(shards), largest / len(shards))
        loudness = loudness * jnp.repeat(jnp.exp(heights), extent[position] // blocks).reshape((-1,) + (1,) * (len(extent) - 1 - position))
    return loudness


def bell_draw(own_key, extent, deviation, limit, split=(), kind=jnp.bfloat16):
    loudness = shard_levels(own_key, extent, split, -0.22, 0.18) if split else 1.0
    values = jax.random.normal(own_key, extent, jnp.float32) * deviation * loudness
    return jnp.minimum(jnp.maximum(values, -limit), limit).astype(kind)


def bell_draw_with(own_key, dims, spread, limit, cuts, heavy, kind=jnp.bfloat16):
    drawn = spread * jax.random.normal(own_key, dims, jnp.float32)
    if cuts:
        drawn = drawn * shard_levels(own_key, dims, cuts, -0.22, 0.18)
    return jnp.clip(strengthened(drawn, jax.random.fold_in(own_key, 3), *heavy), -limit, limit).astype(kind)


def setup_inputs(seed: int = 0) -> dict:
    arg_keys = jax.random.split(jax.random.key(seed), 4)
    return {
        "activations": bell_draw_with(arg_keys[0], (TOKENS, D), (TOKENS ** -0.5), 0.06591797, ((0, 32), (1, 4)), (0, 1, 32, 2.75)),
        "out_grad": bell_draw(arg_keys[1], (TOKENS, D), 1.0, 6.0, ((0, 32), (1, 16))),
        "weight": bell_draw_with(arg_keys[2], (D, D), D ** -0.5, 0.09375, ((0, 16), (1, 4)), (1, 0, 16, 2.0)),
    }


def reference(activations, out_grad, weight):
    block = D // N_GZ

    def add_term(total, k):
        start = (k * block).astype(jnp.int32)
        grads = lax.dynamic_slice_in_dim(out_grad, start, block, 1)
        rows = lax.dynamic_slice_in_dim(weight, start, block, 1)
        term = lax.dot_general(grads, rows, (((1,), (1,)), ((), ())), preferred_element_type=jnp.float32)
        rounded = lax.optimization_barrier(term.astype(jnp.bfloat16))
        return total + rounded.astype(jnp.float32), None

    zeros_dx = jnp.zeros((TOKENS, D), jnp.float32)
    input_grad, _ = lax.scan(add_term, zeros_dx, jnp.arange(N_GZ, dtype=jnp.int32))

    span = TOKENS // N_DP

    def add_share(total, r):
        start = (r * span).astype(jnp.int32)
        inputs = lax.dynamic_slice_in_dim(activations, start, span, 0)
        grads = lax.dynamic_slice_in_dim(out_grad, start, span, 0)
        share = lax.dot_general(inputs, grads, (((0,), (0,)), ((), ())), preferred_element_type=jnp.float32)
        rounded = lax.optimization_barrier(share.astype(jnp.bfloat16))
        return total + rounded.astype(jnp.float32), None

    zeros_dw = jnp.zeros((D, D), jnp.float32)
    weight_grad, _ = lax.scan(add_share, zeros_dw, jnp.arange(N_DP, dtype=jnp.int32))
    return input_grad.astype(jnp.bfloat16), weight_grad
```

```python
import jax
import jax.numpy as jnp
from jax import lax
from jax.sharding import PartitionSpec as P

BF16, F32 = jnp.bfloat16, jnp.float32


def exchange(x, axis, groups=None):
    return lax.all_to_all(x, axis, 0, 0, tiled=True, axis_index_groups=groups)


def gather(x, axis):
    n = lax.axis_size(axis)
    return exchange(jnp.broadcast_to(x[None], (n,) + x.shape), axis)


def total(parts):
    return jnp.sum(parts.astype(F32), axis=0)


def body(a, g, w):
    n = lax.axis_size("gy")
    rows, span = g.shape
    sub = rows // n
    g_all = gather(gather(g, "gy").reshape(n * rows, span), "gx")
    mine = lax.dynamic_slice_in_dim(a, lax.axis_index("gz") * sub, sub, 0)
    got = exchange(mine.reshape(sub, n, span).transpose(1, 0, 2), "gy")
    a_q = gather(got, "gz").transpose(1, 0, 2, 3).reshape(n * rows, span)
    part = lax.dot_general(
        g_all, w.reshape(span, n, span), (((0, 2), (1, 2)), ((), ())), preferred_element_type=F32
    )
    part = part.astype(BF16).reshape(n, n, sub, span).transpose(1, 0, 2, 3)
    dx = total(exchange(part, "gz")).astype(BF16)
    dx = exchange(dx, "gy")
    dx = exchange(dx, "gz").reshape(rows, span)
    share = lax.dot_general(g_all, a_q, (((1,), (0,)), ((), ())), preferred_element_type=F32)
    share = share.astype(BF16).transpose(0, 2, 1).reshape(n, 2, rows, span)
    core = lax.axis_index("dp") % 2
    keep = lax.dynamic_index_in_dim(share, core, 1, keepdims=False)
    send = lax.dynamic_index_in_dim(share, 1 - core, 1, keepdims=False)
    other = lax.ppermute(send, "dp", [(i, i ^ 1) for i in range(8)])
    both = (keep.astype(F32) + other.astype(F32)).astype(BF16)
    dw = total(exchange(both, "dp", [[0, 2, 4, 6], [1, 3, 5, 7]])).astype(BF16)
    swap = [
        ((lo * 2 + c) * 4 + hi, (hi * 2 + c) * 4 + lo)
        for lo in range(4) for c in range(2) for hi in range(4)
    ]
    dw = lax.ppermute(dw, ("dp", "gy"), swap).astype(F32)
    return dx, dw


def solution(mesh):
    return jax.shard_map(
        body,
        mesh=mesh,
        in_specs=(P(("dp", "gy"), "gx"), P(("dp", "gy"), ("gz", "gx")), P(("gx", "gy"), "gz")),
        out_specs=(P(("dp", "gy"), ("gx", "gz")), P(("gx", "dp"), ("gz", "gy"))),
        check_vma=False,
    )
```

```python
import jax
import jax.numpy as jnp
from jax import lax
from jax.experimental import pallas as pl
from jax.experimental.pallas import tpu as pltpu
from jax.sharding import PartitionSpec as P

BF16, F32 = jnp.bfloat16, jnp.float32


def exchange(x, axis):
    return lax.all_to_all(x, axis, 0, 0, tiled=True)


def gather(x, axis):
    n = lax.axis_size(axis)
    return exchange(jnp.broadcast_to(x[None], (n,) + x.shape), axis)


def shift(x, axis, s):
    n = lax.axis_size(axis)
    return lax.ppermute(x, axis, [(i, (i + s) % n) for i in range(n)])


def after(x, *others):
    return pl.pallas_call(
        lambda *refs: None,
        out_shape=jax.ShapeDtypeStruct(x.shape, x.dtype),
        in_specs=[pl.BlockSpec(memory_space=pl.ANY)] * (1 + len(others)),
        out_specs=pl.BlockSpec(memory_space=pl.ANY),
        input_output_aliases={0: 0},
        name="after",
    )(x, *others)


def block(x, i, size, axis):
    return lax.dynamic_slice_in_dim(x, i * size, size, axis)


def turned(parts, first):
    n = len(parts)
    return lax.dynamic_slice_in_dim(jnp.stack(parts * 2), first, n, 0)


def body(a, g, w):
    n = lax.axis_size("gy")
    me, gz = lax.axis_index("gy"), lax.axis_index("gz")
    rows, span = g.shape
    sub, half = rows // n, rows // 2
    w = w.reshape(span, n, span)
    mine = block(a, gz, sub, 0)

    def piece(s):
        return block(mine, lax.rem(me + s, n), span, 1)

    far = piece(2)
    up = shift(jnp.concatenate([g, piece(1), far[: sub // 2]], 0), "gy", 1)
    down = shift(jnp.concatenate([g[half:], g[:half], piece(3), far[sub // 2 :]], 0), "gy", 3)
    b0 = gather(g, "gx")
    via_up = jnp.concatenate([up[:half], up[rows + sub :]], 0)
    via_down = jnp.concatenate([down[:half], down[rows + sub :]], 0)
    far = [shift(after(via_up, b0), "gy", 1), shift(after(via_down, b0), "gy", 3)]
    b13 = gather(jnp.concatenate([up[:rows], down[half:rows], down[:half]], 0), "gx")
    b2 = gather(after(jnp.concatenate([t[:half] for t in far], 0), b13), "gx")
    x = [up[rows : rows + sub], down[rows : rows + sub], jnp.concatenate([t[half:] for t in far], 0)]
    x = jnp.stack(x)
    x = [x] + [shift(x, "gz", s) for s in (1, 2, 3)]
    x = turned([x[0], x[3], x[2], x[1]], lax.rem(n - gz, n))
    acts = x.transpose(1, 0, 2, 3).reshape(3 * rows, span)
    blocks = [b0, b13, b2]
    terms = [
        lax.dot_general(t, w, (((0, 2), (1, 2)), ((), ())), preferred_element_type=F32).astype(BF16) for t in blocks
    ]
    terms = jnp.concatenate(terms, 0).reshape(n, n, sub, span).transpose(1, 0, 2, 3)
    dx = jnp.sum(exchange(terms, "gz").astype(F32), axis=0).astype(BF16)
    dx = turned([dx[0], dx[2], dx[3], dx[1]], lax.rem(n - me, n))
    dx = exchange(exchange(dx, "gy"), "gz").reshape(rows, span)
    acts = [block(a, me, span, 1), acts[: 2 * rows], acts[2 * rows :]]
    dp = lax.axis_index("dp")
    core, lo = lax.rem(dp, 2), lax.div(dp, 2)

    def share(i):
        out = sum(
            lax.dot_general(block(x, i, rows, 1), t, (((0,), (1,)), ((), ())), preferred_element_type=F32)
            for x, t in zip(acts, blocks)
        )
        return out.transpose(1, 0, 2).astype(BF16)

    def partner(x, bit):
        return lax.ppermute(x, "dp", [(i, i ^ bit) for i in range(8)])

    def added(x, y):
        return (x.astype(F32) + y.astype(F32)).astype(BF16)

    other = partner(share(1 - core), 1)
    dw = added(share(core), other).reshape(2, 2, rows, span)
    low, high = lax.rem(lo, 2), lax.div(lo, 2)
    dw = added(block(dw, low, 1, 1), partner(block(dw, 1 - low, 1, 1), 2))[:, 0]
    dw = added(block(dw, high, 1, 0), partner(block(dw, 1 - high, 1, 0), 4))[0]
    swap = [
        ((lo * 2 + c) * 4 + hi, (hi * 2 + c) * 4 + lo)
        for lo in range(4) for c in range(2) for hi in range(4)
    ]
    dw = lax.ppermute(dw, ("dp", "gy"), swap).astype(F32)
    return dx, dw


def solution(mesh):
    return jax.shard_map(
        body,
        mesh=mesh,
        in_specs=(P(("dp", "gy"), "gx"), P(("dp", "gy"), ("gz", "gx")), P(("gx", "gy"), "gz")),
        out_specs=(P(("dp", "gy"), ("gx", "gz")), P(("gx", "dp"), ("gz", "gy"))),
        check_vma=False,
    )
```

```python
import jax
import jax.numpy as jnp
from jax import lax
from jax.experimental import pallas as pl
from jax.experimental.pallas import tpu as pltpu
from jax.sharding import PartitionSpec as P

BF16, F32 = jnp.bfloat16, jnp.float32


def exchange(x, axis):
    return lax.all_to_all(x, axis, 0, 0, tiled=True)


def gather(x, axis):
    n = lax.axis_size(axis)
    return exchange(jnp.broadcast_to(x[None], (n,) + x.shape), axis)


def shift(x, axis, s):
    n = lax.axis_size(axis)
    return lax.ppermute(x, axis, [(i, (i + s) % n) for i in range(n)])


def after(x, *others):
    return pl.pallas_call(
        lambda *refs: None,
        out_shape=jax.ShapeDtypeStruct(x.shape, x.dtype),
        in_specs=[pl.BlockSpec(memory_space=pl.ANY)] * (1 + len(others)),
        out_specs=pl.BlockSpec(memory_space=pl.ANY),
        input_output_aliases={0: 0},
        name="after",
    )(x, *others)


def block(x, i, size, axis):
    return lax.dynamic_slice_in_dim(x, i * size, size, axis)


def turned(parts, first):
    n = len(parts)
    return lax.dynamic_slice_in_dim(jnp.stack(parts * 2), first, n, 0)


def body(a, g, w):
    n = lax.axis_size("gy")
    me, gz = lax.axis_index("gy"), lax.axis_index("gz")
    rows, span = g.shape
    sub, half = rows // n, rows // 2
    w = w.reshape(span, n, span)
    mine = block(a, gz, sub, 0)

    def piece(s):
        return block(mine, lax.rem(me + s, n), span, 1)

    far = piece(2)
    up = shift(jnp.concatenate([g, piece(1), far[: sub // 2]], 0), "gy", 1)
    down = shift(jnp.concatenate([g[half:], g[:half], piece(3), far[sub // 2 :]], 0), "gy", 3)
    b0 = gather(g, "gx")
    via_up = jnp.concatenate([up[:half], up[rows + sub :]], 0)
    via_down = jnp.concatenate([down[:half], down[rows + sub :]], 0)
    far = [shift(after(via_up, b0), "gy", 1), shift(after(via_down, b0), "gy", 3)]
    b13 = gather(jnp.concatenate([up[:rows], down[half:rows], down[:half]], 0), "gx")
    wide = after(jnp.concatenate([t[:half] for t in far], 0), b13[0, :16, :128])
    wide = jnp.broadcast_to(wide[None], (n, rows, span))
    b2 = exchange(wide, "gx")
    x = [up[rows : rows + sub], down[rows : rows + sub], jnp.concatenate([t[half:] for t in far], 0)]
    x = after(jnp.stack(x), wide[0, :16, :128])
    x = [x] + [shift(x, "gz", s) for s in (1, 2, 3)]
    x = turned([x[0], x[3], x[2], x[1]], lax.rem(n - gz, n))
    acts = x.transpose(1, 0, 2, 3).reshape(3 * rows, span)
    blocks = [b0, b13, b2]
    terms = [
        lax.dot_general(t, w, (((0, 2), (1, 2)), ((), ())), preferred_element_type=F32).astype(BF16) for t in blocks
    ]
    acts = [block(a, me, span, 1), acts[: 2 * rows], acts[2 * rows :]]
    dp = lax.axis_index("dp")
    core, lo = lax.rem(dp, 2), lax.div(dp, 2)

    def share(i):
        out = sum(
            lax.dot_general(block(x, i, rows, 1), t, (((0,), (1,)), ((), ())), preferred_element_type=F32)
            for x, t in zip(acts, blocks)
        )
        return out.transpose(1, 0, 2).astype(BF16).reshape(2, 2, rows, span)

    def partner(x, bit):
        return lax.ppermute(x, "dp", [(i, i ^ bit) for i in range(8)])

    def added(*parts):
        return sum(t.astype(F32) for t in parts).astype(BF16)

    first = share(1 - core)
    terms = jnp.concatenate(terms, 0).reshape(n, n, sub, span).transpose(1, 0, 2, 3)
    dx = jnp.sum(exchange(terms, "gz").astype(F32), axis=0).astype(BF16)
    dx = turned([dx[0], dx[2], dx[3], dx[1]], lax.rem(n - me, n))
    dx = exchange(exchange(dx, "gy"), "gz").reshape(rows, span)
    dw = [share(core), partner(first, 1)]
    low, high = lax.rem(lo, 2), lax.div(lo, 2)
    got = partner(added(*(block(t, 1 - low, 1, 1) for t in dw)), 2)
    dw = [block(t, low, 1, 1) for t in dw] + [got]
    got = partner(added(*(block(t, 1 - high, 1, 0) for t in dw)), 4)
    dw = added(*(block(t, high, 1, 0) for t in dw), got)[0, 0]
    swap = [
        ((lo * 2 + c) * 4 + hi, (hi * 2 + c) * 4 + lo)
        for lo in range(4) for c in range(2) for hi in range(4)
    ]
    dw = lax.ppermute(dw, ("dp", "gy"), swap).astype(F32)
    return dx, dw


def solution(mesh):
    return jax.shard_map(
        body,
        mesh=mesh,
        in_specs=(P(("dp", "gy"), "gx"), P(("dp", "gy"), ("gz", "gx")), P(("gx", "gy"), "gz")),
        out_specs=(P(("dp", "gy"), ("gx", "gz")), P(("gx", "dp"), ("gz", "gy"))),
        check_vma=False,
    )
```

```python
import jax
import jax.numpy as jnp
from jax import lax
from jax.experimental import pallas as pl
from jax.experimental.pallas import tpu as pltpu
from jax.sharding import PartitionSpec as P

BF16, F32 = jnp.bfloat16, jnp.float32


def exchange(x, axis):
    return lax.all_to_all(x, axis, 0, 0, tiled=True)


def gather(x, axis):
    n = lax.axis_size(axis)
    return exchange(jnp.broadcast_to(x[None], (n,) + x.shape), axis)


def shift(x, axis, s):
    n = lax.axis_size(axis)
    return lax.ppermute(x, axis, [(i, (i + s) % n) for i in range(n)])


def after(x, *others):
    return pl.pallas_call(
        lambda *refs: None,
        out_shape=jax.ShapeDtypeStruct(x.shape, x.dtype),
        in_specs=[pl.BlockSpec(memory_space=pl.ANY)] * (1 + len(others)),
        out_specs=pl.BlockSpec(memory_space=pl.ANY),
        input_output_aliases={0: 0},
        name="after",
    )(x, *others)


def block(x, i, size, axis):
    return lax.dynamic_slice_in_dim(x, i * size, size, axis)


def turned(parts, first):
    n = len(parts)
    return lax.dynamic_slice_in_dim(jnp.stack(parts * 2), first, n, 0)


def body(a, g, w):
    n = lax.axis_size("gy")
    me, gz = lax.axis_index("gy"), lax.axis_index("gz")
    rows, span = g.shape
    sub, half = rows // n, rows // 2
    w = w.reshape(span, n, span)
    mine = block(a, gz, sub, 0)

    def piece(s):
        return block(mine, lax.rem(me + s, n), span, 1)

    far = piece(2)
    up = shift(jnp.concatenate([g, piece(1), far[: sub // 2]], 0), "gy", 1)
    down = shift(jnp.concatenate([g[half:], g[:half], piece(3), far[sub // 2 :]], 0), "gy", 3)
    b0 = gather(g, "gx")
    via_up = jnp.concatenate([up[:half], up[rows + sub :]], 0)
    via_down = jnp.concatenate([down[:half], down[rows + sub :]], 0)
    far = [shift(after(via_up, b0), "gy", 1), shift(after(via_down, b0), "gy", 3)]
    b13 = gather(jnp.concatenate([up[:rows], down[half:rows], down[:half]], 0), "gx")
    wide = jnp.broadcast_to(jnp.concatenate([t[:half] for t in far], 0)[None], (n, rows, span))
    wide = after(wide, b13[0, :16, :128])
    b2 = exchange(wide, "gx")
    x = [up[rows : rows + sub], down[rows : rows + sub], jnp.concatenate([t[half:] for t in far], 0)]
    x = after(jnp.stack(x), wide[0, :16, :128])
    x = [x] + [shift(x, "gz", s) for s in (1, 2, 3)]
    x = turned([x[0], x[3], x[2], x[1]], lax.rem(n - gz, n))
    acts = x.transpose(1, 0, 2, 3).reshape(3 * rows, span)
    blocks = [b0, b13, b2]
    terms = [
        lax.dot_general(t, w, (((0, 2), (1, 2)), ((), ())), preferred_element_type=F32).astype(BF16) for t in blocks
    ]
    acts = [block(a, me, span, 1), acts[: 2 * rows], acts[2 * rows :]]
    dp = lax.axis_index("dp")
    core, lo = lax.rem(dp, 2), lax.div(dp, 2)

    def share(i):
        out = sum(
            lax.dot_general(block(x, i, rows, 1), t, (((0,), (1,)), ((), ())), preferred_element_type=F32)
            for x, t in zip(acts, blocks)
        )
        return out.transpose(1, 0, 2).astype(BF16).reshape(2, 2, rows, span)

    def partner(x, bit):
        return lax.ppermute(x, "dp", [(i, i ^ bit) for i in range(8)])

    def added(*parts):
        return sum(t.astype(F32) for t in parts).astype(BF16)

    first = share(1 - core)
    terms = jnp.concatenate(terms, 0).reshape(n, n, sub, span)
    dx = [block(terms, gz, 1, 1)] + [shift(block(terms, lax.rem(gz + s, n), 1, 1), "gz", s) for s in (1, 2, 3)]
    dx = sum(t.astype(F32) for t in dx).astype(BF16)[:, 0]
    dx = turned([dx[0], dx[2], dx[3], dx[1]], lax.rem(n - me, n))
    dx = exchange(exchange(dx, "gy"), "gz").reshape(rows, span)
    dw = [share(core), partner(first, 1)]
    low, high = lax.rem(lo, 2), lax.div(lo, 2)
    got = partner(added(*(block(t, 1 - low, 1, 1) for t in dw)), 2)
    dw = [block(t, low, 1, 1) for t in dw] + [got]
    got = partner(added(*(block(t, 1 - high, 1, 0) for t in dw)), 4)
    dw = added(*(block(t, high, 1, 0) for t in dw), got)[0, 0]
    swap = [
        ((lo * 2 + c) * 4 + hi, (hi * 2 + c) * 4 + lo)
        for lo in range(4) for c in range(2) for hi in range(4)
    ]
    dw = lax.ppermute(dw, ("dp", "gy"), swap).astype(F32)
    return dx, dw


def solution(mesh):
    return jax.shard_map(
        body,
        mesh=mesh,
        in_specs=(P(("dp", "gy"), "gx"), P(("dp", "gy"), ("gz", "gx")), P(("gx", "gy"), "gz")),
        out_specs=(P(("dp", "gy"), ("gx", "gz")), P(("gx", "dp"), ("gz", "gy"))),
        check_vma=False,
    )
```

```python
import jax
import jax.numpy as jnp
from jax import lax
from jax.experimental import pallas as pl
from jax.experimental.pallas import tpu as pltpu
from jax.sharding import PartitionSpec as P

BF16, F32 = jnp.bfloat16, jnp.float32


def exchange(x, axis):
    return lax.all_to_all(x, axis, 0, 0, tiled=True)


def gather(x, axis):
    n = lax.axis_size(axis)
    return exchange(jnp.broadcast_to(x[None], (n,) + x.shape), axis)


def shift(x, axis, s):
    n = lax.axis_size(axis)
    return lax.ppermute(x, axis, [(i, (i + s) % n) for i in range(n)])


def after(x, *others):
    return pl.pallas_call(
        lambda *refs: None,
        out_shape=jax.ShapeDtypeStruct(x.shape, x.dtype),
        in_specs=[pl.BlockSpec(memory_space=pl.ANY)] * (1 + len(others)),
        out_specs=pl.BlockSpec(memory_space=pl.ANY),
        input_output_aliases={0: 0},
        name="after",
    )(x, *others)


def block(x, i, size, axis):
    return lax.dynamic_slice_in_dim(x, i * size, size, axis)


def turned(parts, first):
    n = len(parts)
    return lax.dynamic_slice_in_dim(jnp.stack(parts * 2), first, n, 0)


def body(a, g, w):
    n = lax.axis_size("gy")
    me, gz = lax.axis_index("gy"), lax.axis_index("gz")
    rows, span = g.shape
    sub, half = rows // n, rows // 2
    w = w.reshape(span, n, span)
    mine = block(a, gz, sub, 0)

    def piece(s):
        return block(mine, lax.rem(me + s, n), span, 1)

    far = piece(2)
    up = shift(jnp.concatenate([g, piece(1), far[: sub // 2]], 0), "gy", 1)
    down = shift(jnp.concatenate([g, piece(3), far[sub // 2 :]], 0), "gy", 3)
    b0 = gather(g, "gx")
    via_up = jnp.concatenate([up[:half], up[rows + sub :]], 0)
    via_down = jnp.concatenate([down[half:rows], down[rows + sub :]], 0)
    far = [shift(after(via_up, b0), "gy", 1), shift(after(via_down, b0), "gy", 3)]
    b13 = gather(jnp.concatenate([up[:rows], down[:rows]], 0), "gx")
    wide = jnp.broadcast_to(jnp.concatenate([t[:half] for t in far], 0)[None], (n, rows, span))
    wide = after(wide, b13[0, :16, :128])
    b2 = exchange(wide, "gx")
    x = [up[rows : rows + sub], down[rows : rows + sub], jnp.concatenate([t[half:] for t in far], 0)]
    x = after(jnp.stack(x), wide[0, :16, :128])
    x = [x] + [shift(x, "gz", s) for s in (1, 2, 3)]
    x = turned([x[0], x[3], x[2], x[1]], lax.rem(n - gz, n))
    acts = x.transpose(1, 0, 2, 3).reshape(3 * rows, span)
    blocks = [b0, b13, b2]
    terms = [
        lax.dot_general(t, w, (((0, 2), (1, 2)), ((), ())), preferred_element_type=F32).astype(BF16) for t in blocks
    ]
    acts = [block(a, me, span, 1), acts[: 2 * rows], acts[2 * rows :]]
    dp = lax.axis_index("dp")
    core, lo = lax.rem(dp, 2), lax.div(dp, 2)

    def share(i):
        out = sum(
            lax.dot_general(block(x, i, rows, 1), t, (((0,), (1,)), ((), ())), preferred_element_type=F32)
            for x, t in zip(acts, blocks)
        )
        return out.transpose(1, 0, 2).astype(BF16).reshape(2, 2, rows, span)

    def partner(x, bit):
        return lax.ppermute(x, "dp", [(i, i ^ bit) for i in range(8)])

    def added(*parts):
        return sum(t.astype(F32) for t in parts).astype(BF16)

    first = share(1 - core)
    terms = jnp.concatenate(terms, 0).reshape(n, n, sub, span)
    dx = [block(terms, gz, 1, 1)] + [shift(block(terms, lax.rem(gz + s, n), 1, 1), "gz", s) for s in (1, 2, 3)]
    dx = sum(t.astype(F32) for t in dx).astype(BF16)[:, 0]
    dx = turned([dx[0], dx[2], dx[3], dx[1]], lax.rem(n - me, n))
    dx = exchange(exchange(dx, "gy"), "gz").reshape(rows, span)
    dw = [share(core), partner(first, 1)]
    low, high = lax.rem(lo, 2), lax.div(lo, 2)
    got = partner(added(*(block(t, 1 - low, 1, 1) for t in dw)), 2)
    dw = [block(t, low, 1, 1) for t in dw] + [got]
    got = partner(added(*(block(t, 1 - high, 1, 0) for t in dw)), 4)
    dw = added(*(block(t, high, 1, 0) for t in dw), got)[0, 0]
    swap = [
        ((lo * 2 + c) * 4 + hi, (hi * 2 + c) * 4 + lo)
        for lo in range(4) for c in range(2) for hi in range(4)
    ]
    dw = lax.ppermute(dw, ("dp", "gy"), swap).astype(F32)
    return dx, dw


def solution(mesh):
    return jax.shard_map(
        body,
        mesh=mesh,
        in_specs=(P(("dp", "gy"), "gx"), P(("dp", "gy"), ("gz", "gx")), P(("gx", "gy"), "gz")),
        out_specs=(P(("dp", "gy"), ("gx", "gz")), P(("gx", "dp"), ("gz", "gy"))),
        check_vma=False,
    )
```
